32 devices in a mesh: groups: 2 (over y), expert: 4 (over z), hidden: 4 (over x, core).
Axes of the slice: x: 2, y: 2, z: 4, core: 2. Of those that a mesh axis runs over, the one named last changes fastest.
Arguments:
- tokens: bfloat16 [1024, 6144], P(('groups', 'expert'), 'hidden'), parts along dimension 0, may hold values from -6 to 6
- cotangent: bfloat16 [1024, 6144], P(('groups', 'expert'), 'hidden'), parts along dimension 0, may hold values from -6 to 6
- routes: int32 [1024, 4], P(('groups', 'expert')), parts along dimension 0, may hold values from 0 to 15, as said below
- probs: bfloat16 [1024, 4], P(('groups', 'expert')), parts along dimension 0, may hold values from 0.049804688 to 1
- w_gate: bfloat16 [10752, 6144], P('expert', 'hidden'), may hold values from -0.078125 to 0.078125
- w_up: bfloat16 [10752, 6144], P('expert', 'hidden'), may hold values from -0.078125 to 0.078125
- w_down: bfloat16 [10752, 6144], P('expert', 'hidden'), may hold values from -0.0625 to 0.0625
Outputs:
- grad_tokens: bfloat16 [1024, 6144], P(('groups', 'expert'), 'hidden'), parts along dimension 0
- grad_probs: float32 [1024, 4], P(('groups', 'expert')), parts along dimension 0
- grad_gate: bfloat16 [21504, 6144], P(('groups', 'expert'), 'hidden'), parts along dimension 0
- grad_up: bfloat16 [21504, 6144], P(('groups', 'expert'), 'hidden'), parts along dimension 0
- grad_down: bfloat16 [21504, 6144], P(('groups', 'expert'), 'hidden'), parts along dimension 0
The draws below stay inside these ranges and needn't reach their ends.
There are 2 independent parts, one for each index of `groups`. The reference program is written for one: setup_inputs(seed, part) draws one part's arguments, and reference() takes and returns one part's arrays. A program takes and returns all parts, laid end to end along the dimension named above; an argument that names none is the same for every part. Nothing has to cross between parts.
Inputs may be any that keep to these rules, and one draw needn't show every extreme that they name: `routes`: in every row the 4 ids are different. In each aligned block of 128 rows (the rows of one index of the expert axis) expert 0 is named by at most 8 rows, and by exactly 8 rows in at least one block.
All inputs are finite; a program needn't handle non-finite values.
Results may differ from the reference program's by a relative error of at most 0.0065.
Values may be sent and summed in bfloat16 or wider, within the bound.
No kernel may reach another device: no remote copies, remote signals or barrier semaphores. Data moves between devices by JAX's collectives and lax.ppermute only.
A program may use at most 128 MiB of HBM per device.

```python
import jax
import jax.numpy as jnp
from jax import lax

D = 6144
FF = 10752
EXPERTS_ALL = 16
TOPK = 4
TOK_DEV = 128
CAP = 8
TOKENS = 512
N_EXPERT = 4


def draw_routes(key, part):
    key = jax.random.fold_in(key, 11)
    keys = jax.random.split(key, 5)
    blocks = TOKENS // TOK_DEV
    others = EXPERTS_ALL - 1
    scores = jax.random.randint(keys[0], (TOKENS, others), 0, 1 << 20) * others + lax.broadcasted_iota(jnp.int32, (TOKENS, others), 1)
    picks = jnp.argsort(scores, axis=1)[:, :TOPK].astype(jnp.int32) + 1
    counts = jax.random.randint(keys[1], (blocks,), CAP // 2, CAP + 1)
    fullest = jax.random.randint(keys[2], (), 0, blocks)
    counts = jnp.where(jnp.arange(blocks) == fullest, CAP, counts)
    order_scores = jax.random.randint(keys[3], (blocks, TOK_DEV), 0, 1 << 20) * TOK_DEV + lax.broadcasted_iota(jnp.int32, (blocks, TOK_DEV), 1)
    ranks = jnp.argsort(jnp.argsort(order_scores, axis=1), axis=1).astype(jnp.int32)
    taken = (ranks < counts[:, None]).reshape(TOKENS)
    place = jax.random.randint(keys[4], (TOKENS,), 0, TOPK)
    column = lax.broadcasted_iota(jnp.int32, (TOKENS, TOPK), 1)
    return jnp.where(taken[:, None] & (column == place[:, None]), 0, picks).astype(jnp.int32)


def block_scale(own_key, shape, pieces, least, largest):
    loudness, own = 1.0, jax.random.fold_in(own_key, 6)
    for position, shards_of in pieces:
        draws = jnp.exp(jax.random.uniform(jax.random.fold_in(own, position), (shards_of,), jnp.float32, least / len(pieces), largest / len(pieces)))
        loudness = loudness * jnp.repeat(draws, shape[position] // shards_of).reshape([-1 if axis == position else 1 for axis in range(len(shape))])
    return loudness


def normal_values(key, shape, scale, reach, pieces=(), dtype=jnp.bfloat16):
    level = block_scale(key, shape, pieces, -0.22, 0.18) if pieces else 1.0
    result = jax.random.normal(key, shape, jnp.float32) * scale * level
    return jnp.minimum(jnp.maximum(result, -reach), reach).astype(dtype)


def setup_inputs(seed: int = 0, part: int = 0) -> dict:
    seeds = jax.random.split(jax.random.key(seed), 8)
    part_keys = jax.random.split(jax.random.fold_in(seeds[7], part), 8)
    tokens = normal_values(part_keys[0], (TOKENS, D), 1.0, 6.0, ((0, 4), (1, 4)))
    cotangent = normal_values(part_keys[1], (TOKENS, D), 1.0, 6.0, ((0, 4), (1, 4)))
    routes = draw_routes(jax.random.fold_in(jax.random.fold_in(seeds[7], part), 71), part)
    probs = jnp.clip(0.049804688 + 0.9501953 * jax.random.uniform(part_keys[3], (TOKENS, TOPK), jnp.float32) ** block_scale(part_keys[3], (TOKENS, TOPK), ((0, 4),), -0.2, 0.2), 0.049804688, 1.0).astype(jnp.bfloat16)
    w_gate = normal_values(seeds[4], (FF, D), D ** -0.5, 0.078125, ((0, 4), (1, 4)))
    w_up = normal_values(seeds[5], (FF, D), D ** -0.5, 0.078125, ((0, 4), (1, 4)))
    w_down = normal_values(seeds[6], (FF, D), FF ** -0.5, 0.0625, ((0, 4), (1, 4)))
    return {"tokens": tokens, "cotangent": cotangent, "routes": routes, "probs": probs, "w_gate": w_gate, "w_up": w_up, "w_down": w_down}


def reference(tokens, cotangent, routes, probs, w_gate, w_up, w_down):
    chosen = routes == 0
    live = jnp.any(chosen, axis=1)
    route_weight = jnp.sum(jnp.where(chosen, probs.astype(jnp.float32), jnp.float32(0.0)), axis=1)
    count = N_EXPERT * CAP
    index = jnp.argsort(jnp.where(live, 0, 1).astype(jnp.int32), stable=True)[:count].astype(jnp.int32)
    rows_x = tokens[index]
    rows_dy = cotangent[index]
    rows_w = route_weight[index][:, None]
    gate = jnp.dot(rows_x, w_gate.T, preferred_element_type=jnp.float32)
    up = jnp.dot(rows_x, w_up.T, preferred_element_type=jnp.float32)
    sig = jax.nn.sigmoid(gate)
    hidden_act = (gate * sig * up).astype(jnp.bfloat16)
    back_hidden = jnp.dot(rows_dy, w_down.T, preferred_element_type=jnp.float32)
    dots = jnp.sum(hidden_act.astype(jnp.float32) * back_hidden, axis=1)
    token_dots = jnp.zeros((TOKENS,), jnp.float32).at[index].set(dots)
    grad_probs = jnp.where(chosen, token_dots[:, None], jnp.float32(0.0))
    weighted = (rows_w * rows_dy.astype(jnp.float32)).astype(jnp.bfloat16)
    scaled = rows_w * back_hidden
    grad_gate_act = (scaled * up * sig * (1.0 + gate * (1.0 - sig))).astype(jnp.bfloat16)
    grad_up_act = (scaled * gate * sig).astype(jnp.bfloat16)
    rows_grad = jnp.dot(grad_gate_act, w_gate, preferred_element_type=jnp.float32) + jnp.dot(grad_up_act, w_up, preferred_element_type=jnp.float32)
    grad_tokens = jnp.zeros((TOKENS, D), jnp.float32).at[index].add(rows_grad).astype(jnp.bfloat16)
    grad_gate = jnp.dot(grad_gate_act.T, rows_x, preferred_element_type=jnp.float32).astype(jnp.bfloat16)
    grad_up = jnp.dot(grad_up_act.T, rows_x, preferred_element_type=jnp.float32).astype(jnp.bfloat16)
    grad_down = jnp.dot(hidden_act.T, weighted, preferred_element_type=jnp.float32).astype(jnp.bfloat16)
    return (grad_tokens, grad_probs, grad_gate, grad_up, grad_down)
```

```python
import functools

import jax
import jax.numpy as jnp
from jax import lax
from jax.experimental import pallas as pl
from jax.experimental.pallas import tpu as pltpu
from jax.sharding import PartitionSpec as P

CAP = 8
LANES = 128
F32 = jnp.float32
BF16 = jnp.bfloat16
SCALE = 32.0
WAIT_FLOPS = 3 * 10**10
FORWARD_ROWS, OUTER_ROWS, TERM_ROWS = 384, 384, 384
VMEM = pl.BlockSpec(memory_space=pltpu.VMEM)
HBM = pl.BlockSpec(memory_space=pltpu.HBM)


def slot_table(routes, probs, capacity):
    chosen = routes == 0
    live = jnp.any(chosen, axis=1)
    weight = jnp.sum(jnp.where(chosen, probs, jnp.zeros_like(probs)), axis=1)
    order = jnp.cumsum(live.astype(jnp.int32)) - 1
    slots = lax.broadcasted_iota(jnp.int32, (capacity, routes.shape[0]), 0)
    hits = (order[None, :] == slots) & live[None, :]
    slot_weight = jnp.sum(jnp.where(hits, weight[None, :], jnp.zeros_like(weight)[None, :]), axis=1)
    return (chosen, hits, slot_weight)


def contract(left, right, left_dim, right_dim):
    return lax.dot_general(
        left, right, (((left_dim,), (right_dim,)), ((), ())), preferred_element_type=F32
    )


def contract_last(left, right):
    return contract(left, right, 1, 1)


def contract_first(left, right):
    return contract(left, right, 0, 0)


def general_shards(tokens, cotangent, routes, probs, w_gate, w_up, w_down):
    chosen, hits, slot_weight = slot_table(routes, probs, CAP)
    picker = hits.astype(BF16)
    sent_x = jnp.dot(picker, tokens, preferred_element_type=F32).astype(BF16)
    sent_dy = jnp.dot(picker, cotangent, preferred_element_type=F32).astype(BF16)
    rows_x, rows_w = (
        lax.all_gather(sent_x, "expert", axis=0, tiled=True),
        lax.all_gather(slot_weight, "expert", axis=0, tiled=True),
    )
    gate_part = contract_last(rows_x, w_gate)
    up_part = contract_last(rows_x, w_up)
    gate, up = lax.psum((gate_part, up_part), "hidden")
    sig = jax.nn.sigmoid(gate)
    hidden_act = (gate * sig * up).astype(BF16)
    rows_dy = lax.all_gather(sent_dy, "expert", axis=0, tiled=True)
    back_part = contract_last(rows_dy, w_down)
    row_scale = rows_w.astype(F32)[:, None]
    back_hidden = lax.psum(back_part, "hidden")
    scaled = row_scale * back_hidden
    grad_gate_act = (scaled * up * sig * (1.0 + gate * (1.0 - sig))).astype(BF16)
    grad_up_act = (scaled * gate * sig).astype(BF16)
    dots = jnp.sum(hidden_act.astype(F32) * back_hidden, axis=1)
    weighted = (row_scale * rows_dy.astype(F32)).astype(BF16)
    grad_down = contract_first(hidden_act, weighted).astype(BF16)
    grad_gate = contract_first(grad_gate_act, rows_x).astype(BF16)
    grad_up = contract_first(grad_up_act, rows_x).astype(BF16)
    term = jnp.dot(grad_gate_act, w_gate, preferred_element_type=F32) + jnp.dot(
        grad_up_act, w_up, preferred_element_type=F32
    )
    returned, returned_dots = (
        lax.psum_scatter(term, "expert", scatter_dimension=0, tiled=True),
        lax.psum_scatter(dots, "expert", scatter_dimension=0, tiled=True),
    )
    spread = hits.astype(F32)
    grad_tokens = lax.dot_general(
        spread,
        returned,
        (((0,), (0,)), ((), ())),
        precision=lax.Precision.HIGHEST,
        preferred_element_type=F32,
    ).astype(BF16)
    token_dots = jnp.dot(returned_dots, spread, precision=lax.Precision.HIGHEST)
    grad_probs = jnp.where(chosen, token_dots[:, None], F32(0.0))
    return (grad_tokens, grad_probs, grad_gate, grad_up, grad_down)


def slots_of(routes, up_to):
    count = routes.shape[1]
    chosen = routes == 0
    live = jnp.max(jnp.where(chosen, F32(1.0), F32(0.0)), axis=0, keepdims=True)
    live_rows = jnp.broadcast_to(live, (CAP, count))
    order = contract(live_rows.astype(BF16), up_to, 1, 0)
    slots = lax.broadcasted_iota(jnp.int32, (CAP, count), 0).astype(F32) + 1.0
    hits = jnp.where(order == slots, live_rows, F32(0.0))
    return chosen, hits


def triangle_kernel(up_to):
    dims = up_to.shape
    here = lax.broadcasted_iota(jnp.int32, dims, 0) <= lax.broadcasted_iota(jnp.int32, dims, 1)
    up_to[...] = jnp.where(here, F32(1.0), F32(0.0)).astype(BF16)


def pick_kernel(up_to, routes, probs, tokens, cotangent, sent):
    chosen, hits = slots_of(routes[...], up_to[...])
    weight = jnp.sum(jnp.where(chosen, probs[...].astype(F32), F32(0.0)), axis=0, keepdims=True)
    picker = hits.astype(BF16)
    width = tokens.shape[1]
    sent[:, :width] = contract(picker, tokens[...], 1, 0).astype(BF16)
    sent[:, width : 2 * width] = contract(picker, cotangent[...], 1, 0).astype(BF16)
    slot_weight = jnp.sum(hits * weight, axis=1, keepdims=True)
    sent[:, 2 * width :] = jnp.broadcast_to(slot_weight, (CAP, LANES)).astype(BF16)


def ordered(blocks, core):
    half = len(blocks) // 2
    wide = [block.astype(F32) for block in blocks]
    turned = wide[half:] + wide[:half]
    return jnp.concatenate(
        [jnp.where(core == 0, a, b) for a, b in zip(wide, turned)], axis=0
    )


def pieces(size, wanted):
    return [slice(at, min(at + wanted, size)) for at in range(0, size, wanted)]


def forward_spans(spans, x, dy, weights, sums):
    half = x.shape[0] // 2
    for at, span in enumerate(spans):
        mine, theirs = sums[2 * at], sums[2 * at + 1]
        for part in pieces(span.stop - span.start, FORWARD_ROWS):
            rows = slice(span.start + part.start, span.start + part.stop)
            for which, (left, right) in enumerate(zip(weights, (x, x, dy))):
                value = contract(left[rows, :], right, 1, 1).T
                mine[which * half : (which + 1) * half, part] = value[:half]
                theirs[which * half : (which + 1) * half, part] = value[half:]


def forward_first_kernel(
    spans, b3, b2, b1, b0, w_gate, w_up, w_down, rows_x, rows_dy, weighted, scale, *sums
):
    core = lax.rem(lax.axis_index("hidden"), 2)
    width = w_gate.shape[1]
    blocks = ordered([b0[...], b1[...], b2[...], b3[...]], core)
    x = blocks[:, :width].astype(BF16)
    dy32 = blocks[:, width : 2 * width]
    dy = dy32.astype(BF16)
    row_scale = blocks[:, 2 * width :]
    rows_x[...] = x
    rows_dy[...] = dy
    weighted[...] = (row_scale[:, :1] * dy32).astype(BF16)
    scale[...] = row_scale
    forward_spans(spans, x, dy, (w_gate, w_up, w_down), sums)


def forward_next_kernel(spans, x, dy, w_gate, w_up, w_down, *rest):
    sums = rest[-2 * len(spans) :]
    forward_spans(spans, x[...], dy[...], (w_gate, w_up, w_down), sums)


def rounded(value):
    spread = value * 8193.0
    short = spread - (spread - value)
    return jnp.where(jnp.abs(short) < 2.0**-14, F32(0.0), short)


def add_kernel(*refs):
    total = refs[-1]
    at = 0
    for mine, got in zip(refs[:-1:2], refs[1:-1:2]):
        size = mine.shape[1]
        total[:, at : at + size] = rounded((mine[...] + got[...]) * SCALE)
        at += size


def activations(own, other, scale, acts):
    half = own.shape[0] // 3
    row_scale = scale[:half, :1]
    dots = jnp.zeros((half, 1), F32)
    for part in pieces(own.shape[1], 384):
        total = (own[:, part] + other[:, part]) * (1.0 / SCALE)
        gate, up, back = total[:half], total[half : 2 * half], total[2 * half :]
        sig = jax.nn.sigmoid(gate)
        hidden_act = (gate * sig * up).astype(BF16)
        scaled = row_scale * back
        acts[:half, part] = hidden_act
        acts[half : 2 * half, part] = (scaled * up * sig * (1.0 + gate * (1.0 - sig))).astype(BF16)
        acts[2 * half :, part] = (scaled * gate * sig).astype(BF16)
        dots = dots + jnp.sum(hidden_act.astype(F32) * back, axis=1, keepdims=True)
    return dots


def act_first_kernel(own, other, scale, after, acts, dots):
    dots[...] = jnp.broadcast_to(activations(own, other, scale, acts), dots.shape)


def act_last_kernel(own, other, scale, dots_before, after, acts):
    half, width = own.shape[0] // 3, own.shape[1]
    dots = dots_before[:, :1] + activations(own, other, scale, acts)
    high = dots.astype(BF16)
    rest = dots - high.astype(F32)
    middle = rest.astype(BF16)
    low = (rest - middle.astype(F32)).astype(BF16)
    for at, value in enumerate((high, middle, low)):
        acts[at * half : (at + 1) * half, width:] = jnp.broadcast_to(value, (half, LANES))


def both_rows(mine, theirs, at, part):
    half = mine.shape[0] // 3
    here = slice(at * half, (at + 1) * half)
    return jnp.concatenate([mine[here, part], theirs[here, part]], axis=0)


def outer_copies(jobs, staged, sems):
    found = []
    base = 0
    for acts, at, right, out, offset, size in jobs:
        for part in pieces(size, OUTER_ROWS):
            put = slice(base + part.start, base + part.stop)
            target = out.at[slice(offset + part.start, offset + part.stop), :]
            copy = pltpu.make_async_copy(staged.at[put, :], target, sems.at[len(found)])
            found.append((acts, at, right, part, put, copy))
        base += size
    return found


def outer_pieces(jobs, staged, sems):
    found = outer_copies(jobs, staged, sems)
    for acts, at, right, part, put, copy in found:
        staged[put, :] = contract_first(both_rows(*acts, at, part), right[...]).astype(BF16)
        copy.start()
    return [copy for *_, copy in found]


def token_terms(acts, w_gate, w_up, offset, size):
    total = None
    for part in pieces(size, TERM_ROWS):
        rows = slice(offset + part.start, offset + part.stop)
        value = contract(both_rows(*acts, 1, part), w_gate[rows, :], 1, 0)
        value = value + contract(both_rows(*acts, 2, part), w_up[rows, :], 1, 0)
        total = value if total is None else total + value
    return total


def gradients_first_kernel(
    cut, mine, theirs, rows_x, weighted, w_gate, w_up, term, grad_down, grad_gate, staged, sems
):
    core = lax.rem(lax.axis_index("hidden"), 2)
    acts = (mine, theirs)
    jobs = [(acts, 0, weighted, grad_down, 0, cut), (acts, 1, rows_x, grad_gate, 0, cut)]
    copies = outer_pieces(jobs, staged, sems)

    @pl.when(core < 2)
    def products():
        term[...] = token_terms(acts, w_gate, w_up, 0, cut)

    for copy in copies:
        copy.wait()


def up_kernel(size, mine, theirs, rows_x, after, up_here):
    for part in pieces(size, OUTER_ROWS):
        up_here[part, :] = contract_first(both_rows(mine, theirs, 2, part), rows_x[...]).astype(BF16)


def gradients_last_kernel(
    cut, mine, theirs, w_gate, w_up, term, up_here, o0, o1, o2, o3, grad_up, up_sem
):
    core = lax.rem(lax.axis_index("hidden"), 2)
    half = mine.shape[0] // 3
    hidden, width = w_gate.shape
    up_copy = pltpu.make_async_copy(up_here, grad_up.at[slice(0, cut), :], up_sem)
    up_copy.start()

    @pl.when(core < 2)
    def products():
        total = term[...] + token_terms((mine, theirs), w_gate, w_up, cut, hidden - cut)

        def dots_of(ref):
            tail = ref[:, hidden - cut :].astype(F32)
            return tail[:half] + tail[half : 2 * half] + tail[2 * half :]

        dots = jnp.concatenate([dots_of(mine), dots_of(theirs)], axis=0)
        outs = (o0, o1, o2, o3)
        for at, out in enumerate(outs):
            here = slice(at * CAP, (at + 1) * CAP)
            turn = (at + len(outs) // 2) % len(outs)
            there = slice(turn * CAP, (turn + 1) * CAP)
            out[:, :width] = jnp.where(core == 0, total[here], total[there])
            out[:, width:] = jnp.where(core == 0, dots[here], dots[there])

    up_copy.wait()


def gradients_rest_kernel(
    cut, mine, theirs, rows_x, weighted, down_before, gate_before,
    up_here, grad_down, grad_gate, staged, sems,
):
    core = lax.rem(lax.axis_index("hidden"), 2)
    acts, rest = (mine, theirs), grad_gate.shape[0] - cut
    jobs = [(acts, 0, weighted, grad_down, cut, rest), (acts, 1, rows_x, grad_gate, cut, rest)]
    copies = outer_pieces(jobs, staged, sems)

    @pl.when(core < 2)
    def up():
        up_kernel(rest, mine, theirs, rows_x, None, up_here)

    for copy in copies:
        copy.wait()


def place_kernel(
    cut, up_to, routes, r3, r2, r1, r0, up_here, up_before,
    grad_tokens, grad_probs, grad_up, placed, placed_probs, sems,
):
    core = lax.rem(lax.axis_index("hidden"), 2)
    rest = grad_up.shape[0] - cut
    up_copy = pltpu.make_async_copy(up_here, grad_up.at[slice(cut, cut + rest), :], sems.at[0])
    up_copy.start()
    copies = [
        pltpu.make_async_copy(placed, grad_tokens, sems.at[1]),
        pltpu.make_async_copy(placed_probs, grad_probs, sems.at[2]),
    ]

    @pl.when(core < 2)
    def place():
        chosen, hits = slots_of(routes[...], up_to[...])
        total = r0[...] + r1[...] + r2[...] + r3[...]
        width = grad_tokens.shape[1]
        placed[...] = contract_first(hits.astype(BF16), total[:, :width].astype(BF16)).astype(BF16)
        token_dots = jnp.sum(hits * total[:, width : width + 1], axis=0, keepdims=True)
        placed_probs[...] = jnp.where(chosen, token_dots, F32(0.0))

    for copy in copies:
        copy.start()
    up_copy.wait()
    for copy in copies:
        copy.wait()


def shape(dims, dtype):
    return jax.ShapeDtypeStruct(dims, dtype)


def params(mebibytes):
    return pltpu.CompilerParams(vmem_limit_bytes=mebibytes << 20)


def paired_shards(tokens, cotangent, routes, probs, w_gate, w_up, w_down):
    tokens_here, width = tokens.shape
    hidden = w_gate.shape[0]
    rows = 4 * CAP
    half = rows // 2
    routes_t, probs_t = routes.T, probs.T

    def swap(value, axis, bit):
        return lax.ppermute(value, axis, [(i, i ^ bit) for i in range(4)])

    up_to = pl.pallas_call(
        triangle_kernel,
        in_specs=[],
        out_specs=VMEM,
        out_shape=shape((tokens_here, tokens_here), BF16),
        compiler_params=params(1),
        cost_estimate=pl.CostEstimate(flops=WAIT_FLOPS, bytes_accessed=0, transcendentals=0),
        name="triangle",
    )()
    sent = pl.pallas_call(
        pick_kernel,
        in_specs=[VMEM] * 5,
        out_specs=VMEM,
        out_shape=shape((CAP, 2 * width + LANES), BF16),
        compiler_params=params(2),
        name="pick_rows",
    )(up_to, routes_t, probs_t, tokens, cotangent)
    got = [swap(sent, "expert", bit) for bit in (3, 2, 1)]

    def exchange(own):
        return own, swap(own.astype(jnp.float16), "hidden", 2)

    weights = (w_gate, w_up, w_down)
    tiles = hidden // LANES
    cuts = [LANES * at for at in (0, tiles // 2, tiles // 2 + 4, tiles // 2 + 7, tiles)]
    spans = [slice(a, b) for a, b in zip(cuts, cuts[1:])]
    cut = cuts[1]
    rest = hidden - cut

    def cost(products, size):
        return pl.CostEstimate(
            flops=16 * products * rows * size * width, bytes_accessed=0, transcendentals=0
        )

    def call(kernel, name, outs, args, limit=4, **more):
        single = not isinstance(outs, list)
        return pl.pallas_call(
            kernel,
            in_specs=[VMEM] * len(args),
            out_specs=VMEM if single else [VMEM] * len(outs),
            out_shape=outs,
            compiler_params=params(limit),
            name=name,
            **more,
        )(*args)

    def sums(some):
        return [shape((3 * half, span.stop - span.start), F32) for span in some for _ in range(2)]

    rows_x, rows_dy, weighted, scale, mine_a, theirs_a = call(
        functools.partial(forward_first_kernel, spans[:1]),
        "forward_first",
        [shape((rows, width), BF16)] * 3 + [shape((rows, LANES), F32)] + sums(spans[:1]),
        (*got, sent, *weights),
        limit=8,
        cost_estimate=cost(3, cut),
    )
    core_a = swap(theirs_a, "hidden", 1)

    def forward_next(some, after):
        found = call(
            functools.partial(forward_next_kernel, some),
            "forward_next",
            sums(some),
            (rows_x, rows_dy, *weights, *after),
            cost_estimate=cost(3, some[-1].stop - some[0].start),
        )
        return [(m, swap(t, "hidden", 1)) for m, t in zip(found[::2], found[1::2])]

    pairs = forward_next(spans[1:2], ())
    total_a = call(add_kernel, "core_sum_first", shape((3 * half, cut), F32), (mine_a, core_a))
    own_a, other_a = exchange(total_a)
    pairs += forward_next(spans[2:], (own_a,))
    total_b = call(
        add_kernel, "core_sum_last", shape((3 * half, rest), F32), [ref for pair in pairs for ref in pair]
    )
    own_b, other_b = exchange(total_b)

    acts_a, dots_a = call(
        act_first_kernel,
        "activations_first",
        [shape((3 * half, cut), BF16), shape((half, LANES), F32)],
        (own_a, other_a.astype(F32), scale, total_b),
    )
    first = (acts_a, swap(acts_a, "hidden", 1))
    whole = shape((hidden, width), BF16)
    term, down_a, gate_a = pl.pallas_call(
        functools.partial(gradients_first_kernel, cut),
        in_specs=[VMEM] * 6,
        out_specs=[VMEM, HBM, HBM],
        out_shape=[shape((rows, width), F32), whole, whole],
        scratch_shapes=[
            pltpu.VMEM((2 * cut, width), BF16),
            pltpu.SemaphoreType.DMA((2 * len(pieces(cut, OUTER_ROWS)),)),
        ],
        compiler_params=params(12),
        name="gradients_first",
    )(*first, rows_x, weighted, w_gate, w_up)
    other_b, term = lax.optimization_barrier((other_b, term))
    acts_b = call(
        act_last_kernel,
        "activations_last",
        shape((3 * half, rest + LANES), BF16),
        (own_b, other_b.astype(F32), scale, dots_a, term),
    )
    last = (acts_b, swap(acts_b, "hidden", 1))
    up_first = call(
        functools.partial(up_kernel, cut),
        "up_gradient_first",
        shape((cut, width), BF16),
        (*first, rows_x, acts_b),
    )
    *parts, up_a = pl.pallas_call(
        functools.partial(gradients_last_kernel, cut),
        in_specs=[VMEM] * 6,
        out_specs=[VMEM] * 4 + [HBM],
        out_shape=[shape((CAP, width + LANES), F32)] * 4 + [whole],
        scratch_shapes=[pltpu.SemaphoreType.DMA],
        compiler_params=params(4),
        name="gradients_last",
    )(*last, w_gate, w_up, term, up_first)
    back = [swap(parts[bit], "expert", bit) for bit in (3, 2, 1)]

    up_last, grad_down, grad_gate = pl.pallas_call(
        functools.partial(gradients_rest_kernel, cut),
        in_specs=[VMEM] * 4 + [HBM] * 2,
        out_specs=[VMEM, HBM, HBM],
        out_shape=[shape((rest, width), BF16), whole, whole],
        scratch_shapes=[
            pltpu.VMEM((2 * rest, width), BF16),
            pltpu.SemaphoreType.DMA((2 * len(pieces(rest, OUTER_ROWS)),)),
        ],
        input_output_aliases={4: 1, 5: 2},
        compiler_params=params(12),
        cost_estimate=cost(3, rest),
        name="gradients_rest",
    )(*last, rows_x, weighted, down_a, gate_a)

    grad_tokens, grad_probs, grad_up = pl.pallas_call(
        functools.partial(place_kernel, cut),
        in_specs=[VMEM] * 7 + [HBM],
        out_specs=[HBM] * 3,
        out_shape=[shape((tokens_here, width), BF16), shape(routes_t.shape, F32), whole],
        scratch_shapes=[
            pltpu.VMEM((tokens_here, width), BF16),
            pltpu.VMEM(routes_t.shape, F32),
            pltpu.SemaphoreType.DMA((3,)),
        ],
        input_output_aliases={7: 2},
        compiler_params=params(4),
        name="place_rows",
    )(up_to, routes_t, *back, parts[0], up_last, up_a)
    return (grad_tokens, grad_probs.T, grad_gate, grad_up, grad_down)


def solution(mesh):
    placed = (
        P(("groups", "expert"), "hidden"),
        P(("groups", "expert"), "hidden"),
        P(("groups", "expert"), None),
        P(("groups", "expert"), None),
        P("expert", "hidden"),
        P("expert", "hidden"),
        P("expert", "hidden"),
    )

    def shards(tokens, cotangent, routes, probs, w_gate, w_up, w_down):
        paired = mesh.shape["expert"] == 4 and mesh.shape["hidden"] == 4
        paired = paired and w_gate.shape[0] % LANES == 0 and w_gate.shape[1] % LANES == 0
        plan = paired_shards if paired else general_shards
        return plan(tokens, cotangent, routes, probs, w_gate, w_up, w_down)

    return jax.shard_map(
        shards,
        mesh=mesh,
        in_specs=placed,
        out_specs=(
            P(("groups", "expert"), "hidden"),
            P(("groups", "expert"), None),
            P(("groups", "expert"), "hidden"),
            P(("groups", "expert"), "hidden"),
            P(("groups", "expert"), "hidden"),
        ),
        check_vma=False,
    )
```

```python
import functools

import jax
import jax.numpy as jnp
from jax import lax
from jax.experimental import pallas as pl
from jax.experimental.pallas import tpu as pltpu
from jax.sharding import PartitionSpec as P

CAP = 8
LANES = 128
F32 = jnp.float32
BF16 = jnp.bfloat16
SCALE = 32.0
WAIT_FLOPS = 3 * 10**10
FORWARD_ROWS, OUTER_ROWS, TERM_ROWS = 384, 384, 384
VMEM = pl.BlockSpec(memory_space=pltpu.VMEM)
HBM = pl.BlockSpec(memory_space=pltpu.HBM)


def slot_table(routes, probs, capacity):
    chosen = routes == 0
    live = jnp.any(chosen, axis=1)
    weight = jnp.sum(jnp.where(chosen, probs, jnp.zeros_like(probs)), axis=1)
    order = jnp.cumsum(live.astype(jnp.int32)) - 1
    slots = lax.broadcasted_iota(jnp.int32, (capacity, routes.shape[0]), 0)
    hits = (order[None, :] == slots) & live[None, :]
    slot_weight = jnp.sum(jnp.where(hits, weight[None, :], jnp.zeros_like(weight)[None, :]), axis=1)
    return (chosen, hits, slot_weight)


def contract(left, right, left_dim, right_dim):
    return lax.dot_general(
        left, right, (((left_dim,), (right_dim,)), ((), ())), preferred_element_type=F32
    )


def contract_last(left, right):
    return contract(left, right, 1, 1)


def contract_first(left, right):
    return contract(left, right, 0, 0)


def general_shards(tokens, cotangent, routes, probs, w_gate, w_up, w_down):
    chosen, hits, slot_weight = slot_table(routes, probs, CAP)
    picker = hits.astype(BF16)
    sent_x = jnp.dot(picker, tokens, preferred_element_type=F32).astype(BF16)
    sent_dy = jnp.dot(picker, cotangent, preferred_element_type=F32).astype(BF16)
    rows_x, rows_w = (
        lax.all_gather(sent_x, "expert", axis=0, tiled=True),
        lax.all_gather(slot_weight, "expert", axis=0, tiled=True),
    )
    gate_part = contract_last(rows_x, w_gate)
    up_part = contract_last(rows_x, w_up)
    gate, up = lax.psum((gate_part, up_part), "hidden")
    sig = jax.nn.sigmoid(gate)
    hidden_act = (gate * sig * up).astype(BF16)
    rows_dy = lax.all_gather(sent_dy, "expert", axis=0, tiled=True)
    back_part = contract_last(rows_dy, w_down)
    row_scale = rows_w.astype(F32)[:, None]
    back_hidden = lax.psum(back_part, "hidden")
    scaled = row_scale * back_hidden
    grad_gate_act = (scaled * up * sig * (1.0 + gate * (1.0 - sig))).astype(BF16)
    grad_up_act = (scaled * gate * sig).astype(BF16)
    dots = jnp.sum(hidden_act.astype(F32) * back_hidden, axis=1)
    weighted = (row_scale * rows_dy.astype(F32)).astype(BF16)
    grad_down = contract_first(hidden_act, weighted).astype(BF16)
    grad_gate = contract_first(grad_gate_act, rows_x).astype(BF16)
    grad_up = contract_first(grad_up_act, rows_x).astype(BF16)
    term = jnp.dot(grad_gate_act, w_gate, preferred_element_type=F32) + jnp.dot(
        grad_up_act, w_up, preferred_element_type=F32
    )
    returned, returned_dots = (
        lax.psum_scatter(term, "expert", scatter_dimension=0, tiled=True),
        lax.psum_scatter(dots, "expert", scatter_dimension=0, tiled=True),
    )
    spread = hits.astype(F32)
    grad_tokens = lax.dot_general(
        spread,
        returned,
        (((0,), (0,)), ((), ())),
        precision=lax.Precision.HIGHEST,
        preferred_element_type=F32,
    ).astype(BF16)
    token_dots = jnp.dot(returned_dots, spread, precision=lax.Precision.HIGHEST)
    grad_probs = jnp.where(chosen, token_dots[:, None], F32(0.0))
    return (grad_tokens, grad_probs, grad_gate, grad_up, grad_down)


def slots_of(routes, up_to):
    count = routes.shape[1]
    chosen = routes == 0
    live = jnp.max(jnp.where(chosen, F32(1.0), F32(0.0)), axis=0, keepdims=True)
    live_rows = jnp.broadcast_to(live, (CAP, count))
    order = contract(live_rows.astype(BF16), up_to, 1, 0)
    slots = lax.broadcasted_iota(jnp.int32, (CAP, count), 0).astype(F32) + 1.0
    hits = jnp.where(order == slots, live_rows, F32(0.0))
    return chosen, hits


def triangle_kernel(up_to):
    dims = up_to.shape
    here = lax.broadcasted_iota(jnp.int32, dims, 0) <= lax.broadcasted_iota(jnp.int32, dims, 1)
    up_to[...] = jnp.where(here, F32(1.0), F32(0.0)).astype(BF16)


def slots_kernel(up_to, routes, hits):
    hits[...] = slots_of(routes[...], up_to[...])[1]


def pick_kernel(hits_in, routes, probs, tokens, cotangent, sent):
    chosen, hits = routes[...] == 0, hits_in[...]
    weight = jnp.sum(jnp.where(chosen, probs[...].astype(F32), F32(0.0)), axis=0, keepdims=True)
    picker = hits.astype(BF16)
    width = tokens.shape[1]
    sent[:, :width] = contract(picker, tokens[...], 1, 0).astype(BF16)
    sent[:, width : 2 * width] = contract(picker, cotangent[...], 1, 0).astype(BF16)
    slot_weight = jnp.sum(hits * weight, axis=1, keepdims=True)
    sent[:, 2 * width :] = jnp.broadcast_to(slot_weight, (CAP, LANES)).astype(BF16)


def ordered(blocks, core):
    half = len(blocks) // 2
    wide = [block.astype(F32) for block in blocks]
    turned = wide[half:] + wide[:half]
    return jnp.concatenate(
        [jnp.where(core == 0, a, b) for a, b in zip(wide, turned)], axis=0
    )


def pieces(size, wanted):
    return [slice(at, min(at + wanted, size)) for at in range(0, size, wanted)]


def forward_spans(spans, x, dy, weights, sums):
    half = x.shape[0] // 2
    for at, span in enumerate(spans):
        mine, theirs = sums[2 * at], sums[2 * at + 1]
        for part in pieces(span.stop - span.start, FORWARD_ROWS):
            rows = slice(span.start + part.start, span.start + part.stop)
            for which, (left, right) in enumerate(zip(weights, (x, x, dy))):
                value = contract(left[rows, :], right, 1, 1).T
                mine[which * half : (which + 1) * half, part] = value[:half]
                theirs[which * half : (which + 1) * half, part] = value[half:]


def forward_first_kernel(
    spans, b3, b2, b1, b0, w_gate, w_up, w_down, rows_x, rows_dy, weighted, scale, *sums
):
    core = lax.rem(lax.axis_index("hidden"), 2)
    width = w_gate.shape[1]
    blocks = ordered([b0[...], b1[...], b2[...], b3[...]], core)
    x = blocks[:, :width].astype(BF16)
    dy32 = blocks[:, width : 2 * width]
    dy = dy32.astype(BF16)
    row_scale = blocks[:, 2 * width :]
    rows_x[...] = x
    rows_dy[...] = dy
    weighted[...] = (row_scale[:, :1] * dy32).astype(BF16)
    scale[...] = row_scale
    forward_spans(spans, x, dy, (w_gate, w_up, w_down), sums)


def forward_next_kernel(spans, x, dy, w_gate, w_up, w_down, *rest):
    sums = rest[-2 * len(spans) :]
    forward_spans(spans, x[...], dy[...], (w_gate, w_up, w_down), sums)


def rounded(value):
    spread = value * 8193.0
    short = spread - (spread - value)
    return jnp.where(jnp.abs(short) < 2.0**-14, F32(0.0), short)


def add_kernel(*refs):
    total = refs[-1]
    at = 0
    for mine, got in zip(refs[:-1:2], refs[1:-1:2]):
        size = mine.shape[1]
        total[:, at : at + size] = rounded((mine[...] + got[...]) * SCALE)
        at += size


def activations(own, other, scale, acts):
    half = own.shape[0] // 3
    row_scale = scale[:half, :1]
    dots = jnp.zeros((half, 1), F32)
    for part in pieces(own.shape[1], 384):
        total = (own[:, part] + other[:, part]) * (1.0 / SCALE)
        gate, up, back = total[:half], total[half : 2 * half], total[2 * half :]
        sig = jax.nn.sigmoid(gate)
        hidden_act = (gate * sig * up).astype(BF16)
        scaled = row_scale * back
        acts[:half, part] = hidden_act
        acts[half : 2 * half, part] = (scaled * up * sig * (1.0 + gate * (1.0 - sig))).astype(BF16)
        acts[2 * half :, part] = (scaled * gate * sig).astype(BF16)
        dots = dots + jnp.sum(hidden_act.astype(F32) * back, axis=1, keepdims=True)
    return dots


def act_first_kernel(own, other, scale, after, acts, dots):
    dots[...] = jnp.broadcast_to(activations(own, other, scale, acts), dots.shape)


def act_last_kernel(own, other, scale, dots_before, after, acts):
    half, width = own.shape[0] // 3, own.shape[1]
    dots = dots_before[:, :1] + activations(own, other, scale, acts)
    high = dots.astype(BF16)
    rest = dots - high.astype(F32)
    middle = rest.astype(BF16)
    low = (rest - middle.astype(F32)).astype(BF16)
    for at, value in enumerate((high, middle, low)):
        acts[at * half : (at + 1) * half, width:] = jnp.broadcast_to(value, (half, LANES))


def both_rows(mine, theirs, at, part):
    half = mine.shape[0] // 3
    here = slice(at * half, (at + 1) * half)
    return jnp.concatenate([mine[here, part], theirs[here, part]], axis=0)


def outer_copies(jobs, staged, sems):
    found = []
    base = 0
    for acts, at, right, out, offset, size in jobs:
        for part in pieces(size, OUTER_ROWS):
            put = slice(base + part.start, base + part.stop)
            target = out.at[slice(offset + part.start, offset + part.stop), :]
            copy = pltpu.make_async_copy(staged.at[put, :], target, sems.at[len(found)])
            found.append((acts, at, right, part, put, copy))
        base += size
    return found


def outer_pieces(jobs, staged, sems):
    found = outer_copies(jobs, staged, sems)
    for acts, at, right, part, put, copy in found:
        staged[put, :] = contract_first(both_rows(*acts, at, part), right[...]).astype(BF16)
        copy.start()
    return [copy for *_, copy in found]


def token_terms(acts, w_gate, w_up, offset, size):
    total = None
    for part in pieces(size, TERM_ROWS):
        rows = slice(offset + part.start, offset + part.stop)
        value = contract(both_rows(*acts, 1, part), w_gate[rows, :], 1, 0)
        value = value + contract(both_rows(*acts, 2, part), w_up[rows, :], 1, 0)
        total = value if total is None else total + value
    return total


def gradients_first_kernel(
    cut, mine, theirs, rows_x, weighted, w_gate, w_up, term, grad_down, grad_gate, staged, sems
):
    core = lax.rem(lax.axis_index("hidden"), 2)
    acts = (mine, theirs)
    jobs = [(acts, 0, weighted, grad_down, 0, cut), (acts, 1, rows_x, grad_gate, 0, cut)]
    copies = outer_pieces(jobs, staged, sems)

    @pl.when(core < 2)
    def products():
        term[...] = token_terms(acts, w_gate, w_up, 0, cut)

    for copy in copies:
        copy.wait()


def up_kernel(size, mine, theirs, rows_x, after, up_here):
    for part in pieces(size, OUTER_ROWS):
        up_here[part, :] = contract_first(both_rows(mine, theirs, 2, part), rows_x[...]).astype(BF16)


def gradients_last_kernel(
    cut, mine, theirs, w_gate, w_up, term, up_here, o0, o1, o2, o3, grad_up, up_sem
):
    core = lax.rem(lax.axis_index("hidden"), 2)
    half = mine.shape[0] // 3
    hidden, width = w_gate.shape
    up_copy = pltpu.make_async_copy(up_here, grad_up.at[slice(0, cut), :], up_sem)
    up_copy.start()

    @pl.when(core < 2)
    def products():
        total = term[...] + token_terms((mine, theirs), w_gate, w_up, cut, hidden - cut)

        def dots_of(ref):
            tail = ref[:, hidden - cut :].astype(F32)
            return tail[:half] + tail[half : 2 * half] + tail[2 * half :]

        dots = jnp.concatenate([dots_of(mine), dots_of(theirs)], axis=0)
        outs = (o0, o1, o2, o3)
        for at, out in enumerate(outs):
            here = slice(at * CAP, (at + 1) * CAP)
            turn = (at + len(outs) // 2) % len(outs)
            there = slice(turn * CAP, (turn + 1) * CAP)
            out[:, :width] = jnp.where(core == 0, total[here], total[there])
            out[:, width:] = jnp.where(core == 0, dots[here], dots[there])

    up_copy.wait()


def gradients_rest_kernel(
    cut, mine, theirs, rows_x, weighted, down_before, gate_before,
    up_here, grad_down, grad_gate, staged, sems,
):
    core = lax.rem(lax.axis_index("hidden"), 2)
    acts, rest = (mine, theirs), grad_gate.shape[0] - cut
    jobs = [(acts, 0, weighted, grad_down, cut, rest), (acts, 1, rows_x, grad_gate, cut, rest)]
    copies = outer_pieces(jobs, staged, sems)

    @pl.when(core < 2)
    def up():
        up_kernel(rest, mine, theirs, rows_x, None, up_here)

    for copy in copies:
        copy.wait()


def place_kernel(
    cut, hits, routes, r2, r3, r1, r0, up_here, up_before,
    grad_tokens, grad_probs, grad_up, placed, placed_probs, sems,
):
    core = lax.rem(lax.axis_index("hidden"), 2)
    rest = grad_up.shape[0] - cut
    up_copy = pltpu.make_async_copy(up_here, grad_up.at[slice(cut, cut + rest), :], sems.at[0])
    up_copy.start()
    copies = [
        pltpu.make_async_copy(placed, grad_tokens, sems.at[1]),
        pltpu.make_async_copy(placed_probs, grad_probs, sems.at[2]),
    ]

    @pl.when(core < 2)
    def place():
        chosen = routes[...] == 0
        total = r0[...] + r1[...] + r2[...] + r3[...]
        width = grad_tokens.shape[1]
        placed[...] = contract_first(hits[...].astype(BF16), total[:, :width].astype(BF16)).astype(BF16)
        token_dots = jnp.sum(hits[...] * total[:, width : width + 1], axis=0, keepdims=True)
        placed_probs[...] = jnp.where(chosen, token_dots, F32(0.0))

    for copy in copies:
        copy.start()
    up_copy.wait()
    for copy in copies:
        copy.wait()


def shape(dims, dtype):
    return jax.ShapeDtypeStruct(dims, dtype)


def params(mebibytes):
    return pltpu.CompilerParams(vmem_limit_bytes=mebibytes << 20)


def paired_shards(tokens, cotangent, routes, probs, w_gate, w_up, w_down):
    tokens_here, width = tokens.shape
    hidden = w_gate.shape[0]
    rows = 4 * CAP
    half = rows // 2
    routes_t, probs_t = routes.T, probs.T

    def swap(value, axis, bit):
        return lax.ppermute(value, axis, [(i, i ^ bit) for i in range(4)])

    up_to = pl.pallas_call(
        triangle_kernel,
        in_specs=[],
        out_specs=VMEM,
        out_shape=shape((tokens_here, tokens_here), BF16),
        compiler_params=params(1),
        cost_estimate=pl.CostEstimate(flops=WAIT_FLOPS, bytes_accessed=0, transcendentals=0),
        name="triangle",
    )()
    hits = pl.pallas_call(
        slots_kernel,
        in_specs=[VMEM] * 2,
        out_specs=VMEM,
        out_shape=shape((CAP, tokens_here), F32),
        compiler_params=params(1),
        name="find_slots",
    )(up_to, routes_t)
    sent = pl.pallas_call(
        pick_kernel,
        in_specs=[VMEM] * 5,
        out_specs=VMEM,
        out_shape=shape((CAP, 2 * width + LANES), BF16),
        compiler_params=params(2),
        name="pick_rows",
    )(hits, routes_t, probs_t, tokens, cotangent)
    got = [swap(sent, "expert", bit) for bit in (3, 2, 1)]

    def exchange(own):
        return own, swap(own.astype(jnp.float16), "hidden", 2)

    weights = (w_gate, w_up, w_down)
    tiles = hidden // LANES
    cuts = [LANES * at for at in (0, tiles // 2, tiles // 2 + 4, tiles // 2 + 7, tiles)]
    spans = [slice(a, b) for a, b in zip(cuts, cuts[1:])]
    cut = cuts[1]
    rest = hidden - cut

    def cost(products, size):
        return pl.CostEstimate(
            flops=16 * products * rows * size * width, bytes_accessed=0, transcendentals=0
        )

    def call(kernel, name, outs, args, limit=4, **more):
        single = not isinstance(outs, list)
        return pl.pallas_call(
            kernel,
            in_specs=[VMEM] * len(args),
            out_specs=VMEM if single else [VMEM] * len(outs),
            out_shape=outs,
            compiler_params=params(limit),
            name=name,
            **more,
        )(*args)

    def sums(some):
        return [shape((3 * half, span.stop - span.start), F32) for span in some for _ in range(2)]

    rows_x, rows_dy, weighted, scale, mine_a, theirs_a = call(
        functools.partial(forward_first_kernel, spans[:1]),
        "forward_first",
        [shape((rows, width), BF16)] * 3 + [shape((rows, LANES), F32)] + sums(spans[:1]),
        (*got, sent, *weights),
        limit=8,
        cost_estimate=cost(3, cut),
    )
    core_a = swap(theirs_a, "hidden", 1)

    def forward_next(some, after):
        found = call(
            functools.partial(forward_next_kernel, some),
            "forward_next",
            sums(some),
            (rows_x, rows_dy, *weights, *after),
            cost_estimate=cost(3, some[-1].stop - some[0].start),
        )
        return [(m, swap(t, "hidden", 1)) for m, t in zip(found[::2], found[1::2])]

    pairs = forward_next(spans[1:2], ())
    total_a = call(add_kernel, "core_sum_first", shape((3 * half, cut), F32), (mine_a, core_a))
    own_a, other_a = exchange(total_a)
    pairs += forward_next(spans[2:], (own_a,))
    total_b = call(
        add_kernel, "core_sum_last", shape((3 * half, rest), F32), [ref for pair in pairs for ref in pair]
    )
    own_b, other_b = exchange(total_b)

    acts_a, dots_a = call(
        act_first_kernel,
        "activations_first",
        [shape((3 * half, cut), BF16), shape((half, LANES), F32)],
        (own_a, other_a.astype(F32), scale, total_b),
    )
    first = (acts_a, swap(acts_a, "hidden", 1))
    whole = shape((hidden, width), BF16)
    term, down_a, gate_a = pl.pallas_call(
        functools.partial(gradients_first_kernel, cut),
        in_specs=[VMEM] * 6,
        out_specs=[VMEM, HBM, HBM],
        out_shape=[shape((rows, width), F32), whole, whole],
        scratch_shapes=[
            pltpu.VMEM((2 * cut, width), BF16),
            pltpu.SemaphoreType.DMA((2 * len(pieces(cut, OUTER_ROWS)),)),
        ],
        compiler_params=params(12),
        name="gradients_first",
    )(*first, rows_x, weighted, w_gate, w_up)
    other_b, term = lax.optimization_barrier((other_b, term))
    acts_b = call(
        act_last_kernel,
        "activations_last",
        shape((3 * half, rest + LANES), BF16),
        (own_b, other_b.astype(F32), scale, dots_a, term),
    )
    last = (acts_b, swap(acts_b, "hidden", 1))
    up_first = call(
        functools.partial(up_kernel, cut),
        "up_gradient_first",
        shape((cut, width), BF16),
        (*first, rows_x, acts_b),
    )
    *parts, up_a = pl.pallas_call(
        functools.partial(gradients_last_kernel, cut),
        in_specs=[VMEM] * 6,
        out_specs=[VMEM] * 4 + [HBM],
        out_shape=[shape((CAP, width + LANES), F32)] * 4 + [whole],
        scratch_shapes=[pltpu.SemaphoreType.DMA],
        compiler_params=params(4),
        name="gradients_last",
    )(*last, w_gate, w_up, term, up_first)
    back = [swap(parts[bit], "expert", bit) for bit in (2, 3, 1)]

    up_last, grad_down, grad_gate = pl.pallas_call(
        functools.partial(gradients_rest_kernel, cut),
        in_specs=[VMEM] * 4 + [HBM] * 2,
        out_specs=[VMEM, HBM, HBM],
        out_shape=[shape((rest, width), BF16), whole, whole],
        scratch_shapes=[
            pltpu.VMEM((2 * rest, width), BF16),
            pltpu.SemaphoreType.DMA((2 * len(pieces(rest, OUTER_ROWS)),)),
        ],
        input_output_aliases={4: 1, 5: 2},
        compiler_params=params(12),
        cost_estimate=cost(3, rest),
        name="gradients_rest",
    )(*last, rows_x, weighted, down_a, gate_a)

    grad_tokens, grad_probs, grad_up = pl.pallas_call(
        functools.partial(place_kernel, cut),
        in_specs=[VMEM] * 7 + [HBM],
        out_specs=[HBM] * 3,
        out_shape=[shape((tokens_here, width), BF16), shape(routes_t.shape, F32), whole],
        scratch_shapes=[
            pltpu.VMEM((tokens_here, width), BF16),
            pltpu.VMEM(routes_t.shape, F32),
            pltpu.SemaphoreType.DMA((3,)),
        ],
        input_output_aliases={7: 2},
        compiler_params=params(4),
        name="place_rows",
    )(hits, routes_t, *back, parts[0], up_last, up_a)
    return (grad_tokens, grad_probs.T, grad_gate, grad_up, grad_down)


def solution(mesh):
    placed = (
        P(("groups", "expert"), "hidden"),
        P(("groups", "expert"), "hidden"),
        P(("groups", "expert"), None),
        P(("groups", "expert"), None),
        P("expert", "hidden"),
        P("expert", "hidden"),
        P("expert", "hidden"),
    )

    def shards(tokens, cotangent, routes, probs, w_gate, w_up, w_down):
        paired = mesh.shape["expert"] == 4 and mesh.shape["hidden"] == 4
        paired = paired and w_gate.shape[0] % LANES == 0 and w_gate.shape[1] % LANES == 0
        plan = paired_shards if paired else general_shards
        return plan(tokens, cotangent, routes, probs, w_gate, w_up, w_down)

    return jax.shard_map(
        shards,
        mesh=mesh,
        in_specs=placed,
        out_specs=(
            P(("groups", "expert"), "hidden"),
            P(("groups", "expert"), None),
            P(("groups", "expert"), "hidden"),
            P(("groups", "expert"), "hidden"),
            P(("groups", "expert"), "hidden"),
        ),
        check_vma=False,
    )
```
